128 devices in a mesh: prow: 8 (over y, core), pcol: 16 (over z, x).
Axes of the slice: x: 4, y: 4, z: 4, core: 2. Of those that a mesh axis runs over, the one named last changes fastest.
Arguments:
- covariance: bfloat16 [2, 4, 8, 512, 2, 16, 512], P(None, None, 'prow', None, None, 'pcol'), may hold values from 0 to 2, as said below
Outputs:
- factored: float32 [2, 4, 8, 512, 2, 16, 512], P(None, None, 'prow', None, None, 'pcol')
The draws below stay inside these ranges and needn't reach their ends.
Inputs may be any that keep to these rules, and one draw needn't show every extreme that they name: For each candidate a symmetric positive definite Matern covariance of scattered observations (smoothness 1/2, 3/2 or 5/2) plus a positive nugget on the diagonal.
All inputs are finite; a program needn't handle non-finite values.
Results may differ from the reference program's by a relative error of at most 0.0019.
Values may be sent and summed in bfloat16 or wider, within the bound.
No kernel may reach another device: no remote copies, remote signals or barrier semaphores. Data moves between devices by JAX's collectives and lax.ppermute only.
A program may use at most 192 MiB of HBM per device.

```python
import math
import jax
import jax.numpy as jnp
from jax import lax

NB = 512
FACTORED = 2
CAND = 2
LC = 2
LR = 4
M = 16384


def draw_covariance(key, part):
    subkeys = jax.random.split(jax.random.fold_in(key, 11), 5)
    side_length = math.sqrt(M)
    coords = jax.random.uniform(subkeys[0], (CAND, 2, M), jnp.float32) * side_length
    length = side_length * jnp.exp(jax.random.uniform(subkeys[1], (CAND,), jnp.float32, math.log(0.08), math.log(0.25)))
    variance = jnp.exp(jax.random.uniform(subkeys[2], (CAND,), jnp.float32, math.log(0.7), math.log(1.4)))
    nugget = jax.random.uniform(subkeys[3], (CAND,), jnp.float32, 0.3, 0.5)
    smooth = jax.random.randint(subkeys[4], (CAND,), 0, 3)

    def one_block(block_index):
        first_row = block_index * NB
        near_points = lax.dynamic_slice_in_dim(coords, first_row, NB, 2)
        delta_x = near_points[:, 0, :, None] - coords[:, 0, None, :]
        delta_y = near_points[:, 1, :, None] - coords[:, 1, None, :]
        scaled = jnp.sqrt(delta_x * delta_x + delta_y * delta_y) / length[:, None, None]
        kernel_half = jnp.exp(-scaled)
        kernel_three = (1.0 + math.sqrt(3.0) * scaled) * jnp.exp(-math.sqrt(3.0) * scaled)
        kernel_five = (1.0 + math.sqrt(5.0) * scaled + 5.0 * scaled * scaled / 3.0) * jnp.exp(-math.sqrt(5.0) * scaled)
        code = smooth[:, None, None]
        kernel = jnp.where(code == 0, kernel_half, jnp.where(code == 1, kernel_three, kernel_five))
        same_point = (first_row + jnp.arange(NB))[:, None] == jnp.arange(M)[None, :]
        entries = variance[:, None, None] * kernel + jnp.where(same_point[None], nugget[:, None, None], 0.0)
        return entries.astype(jnp.bfloat16)
    stacked = lax.map(one_block, jnp.arange(M // NB))
    whole = jnp.transpose(stacked, (1, 0, 2, 3)).reshape(CAND, M, M)
    return whole.reshape(CAND, LR, M // (LR * NB), NB, LC, M // (LC * NB), NB)


def setup_inputs(seed: int = 0) -> dict:
    arg_keys = jax.random.split(jax.random.key(seed), 2)
    return {
        "covariance": draw_covariance(jax.random.fold_in(arg_keys[1], 71), 0),
    }


def factor_one(matrix):
    matrix = matrix.astype(jnp.float32)
    row_index = jnp.arange(M)
    columns = []
    for tile_step in range(FACTORED):
        start_row = tile_step * NB
        diag_block = matrix[start_row:start_row + NB, start_row:start_row + NB]
        lower_factor = jnp.linalg.cholesky(diag_block)
        solved = lax.linalg.triangular_solve(lower_factor, matrix[:, start_row:start_row + NB], left_side=False, lower=True, transpose_a=True)
        below_mask = (row_index >= start_row + NB)[:, None]
        panel_rows = jnp.where(below_mask, solved, 0.0)
        columns.append(panel_rows.at[start_row:start_row + NB].set(lower_factor))
        rounded = panel_rows.astype(jnp.bfloat16)
        matrix = matrix - jnp.dot(rounded.astype(jnp.float32), rounded.T.astype(jnp.float32), preferred_element_type=jnp.float32)
    factored_cols = FACTORED * NB
    upper_mask = (row_index < factored_cols)[:, None]
    right_part = jnp.where(upper_mask, 0.0, matrix[:, factored_cols:])
    return jnp.concatenate(columns + [right_part], axis=1)

def reference(covariance):
    whole = covariance.reshape(CAND, M, M)
    result = jnp.stack([factor_one(whole[candidate]) for candidate in range(CAND)])
    return result.reshape(covariance.shape)
```

```python
import jax
import jax.numpy as jnp
from jax import lax
from jax.experimental import pallas as pl
from jax.experimental.pallas import tpu as pltpu
from jax.sharding import PartitionSpec as P

TILE = 512
CAND = 2
BASE = 64
F32 = jnp.float32
BF16 = jnp.bfloat16


def lane_pick(value, column):
    lane = lax.broadcasted_iota(jnp.int32, (8, 128), 1)
    index = jnp.where(lane < BASE, column, BASE + column)
    return jnp.take_along_axis(value, index, axis=1, mode="promise_in_bounds")


def row_spread(value, row):
    return jnp.broadcast_to(value[row : row + 1, :], (8, 128))


def factor_base(groups):
    lane = lax.broadcasted_iota(jnp.int32, (8, 128), 1)
    half = jnp.where(lane < BASE, lane, lane - BASE)
    sub = lax.broadcasted_iota(jnp.int32, (8, 128), 0)
    work = list(groups)
    inverse = [jnp.where(half == sub + 8 * i, 1.0, 0.0).astype(F32) for i in range(8)]
    lower = [jnp.zeros((8, 128), F32) for _ in range(8)]
    for i in range(8):
        rows = [row_spread(work[i], j) for j in range(8)]
        inv_rows = [row_spread(inverse[i], j) for j in range(8)]
        entry = [
            [lane_pick(rows[j], 8 * i + m) if m >= j else None for m in range(8)] for j in range(8)
        ]
        factor = [[None] * 8 for _ in range(8)]
        scale = [None] * 8
        for j in range(8):
            scale[j] = lax.rsqrt(entry[j][j])
            for m in range(j + 1, 8):
                factor[m][j] = entry[j][m] * scale[j]
            for a in range(j + 1, 8):
                for b in range(a, 8):
                    entry[a][b] = entry[a][b] - factor[a][j] * factor[b][j]
            rows[j] = rows[j] * scale[j]
            inv_rows[j] = inv_rows[j] * scale[j]
            for m in range(j + 1, 8):
                rows[m] = rows[m] - factor[m][j] * rows[j]
                inv_rows[m] = inv_rows[m] - factor[m][j] * inv_rows[j]
        merged = inv_rows[0]
        for j in range(1, 8):
            merged = jnp.where(sub == j, inv_rows[j], merged)
        inverse[i] = merged
        for q in range(i, 8):
            column = [lane_pick(work[q], 8 * i + j) for j in range(8)]
            for j in range(8):
                column[j] = column[j] * scale[j]
                for m in range(j + 1, 8):
                    column[m] = column[m] - column[j] * factor[m][j]
                here = half == 8 * i + j
                if q == i:
                    here = here & (sub >= j)
                lower[q] = jnp.where(here, column[j], lower[q])
            if q > i:
                for j in range(8):
                    work[q] = work[q] - column[j] * rows[j]
                    inverse[q] = inverse[q] - column[j] * inv_rows[j]
    return lower, inverse


def dot_high(left, right, right_dim):
    return lax.dot_general(
        left,
        right,
        (((1,), (right_dim,)), ((), ())),
        precision=lax.Precision.HIGHEST,
        preferred_element_type=F32,
    )


def factor_block(work, low, inv, start, size):
    if size == BASE:
        window = start // 128 * 128
        odd = start % 128 != 0
        rows = slice(start, start + BASE)
        lane = lax.broadcasted_iota(jnp.int32, (BASE, 128), 1)
        first = work[0, rows, window : window + 128]
        second = work[1, rows, window : window + 128]
        if odd:
            first = pltpu.roll(first, BASE, 1)
        else:
            second = pltpu.roll(second, BASE, 1)
        both = jnp.where(lane < BASE, first, second)
        lower, inverse = factor_base([both[8 * i : 8 * i + 8, :] for i in range(8)])
        for target, parts in ((low, lower), (inv, inverse)):
            value = jnp.concatenate(parts, 0)
            rolled = pltpu.roll(value, BASE, 1)
            cols = slice(start, start + BASE)
            if odd:
                target[0, rows, cols] = rolled[:, BASE:]
                target[1, rows, cols] = value[:, BASE:]
            else:
                target[0, rows, cols] = value[:, :BASE]
                target[1, rows, cols] = rolled[:, :BASE]
        return
    half = size // 2
    top = slice(start, start + half)
    bottom = slice(start + half, start + size)
    factor_block(work, low, inv, start, half)
    for c in range(CAND):
        below = dot_high(work[c, bottom, top], inv[c, top, top], 1)
        low[c, bottom, top] = below
        work[c, bottom, bottom] = work[c, bottom, bottom] - dot_high(below, below, 1)
    factor_block(work, low, inv, start + half, half)
    for c in range(CAND):
        inner = dot_high(low[c, bottom, top], inv[c, top, top], 0)
        inv[c, bottom, top] = -dot_high(inv[c, bottom, bottom], inner, 0)


def split_store(inv, high_ref, rest_ref):
    for c in range(CAND):
        value = inv[c]
        high = value.astype(BF16)
        high_ref[c] = high
        rest_ref[c] = (value - high.astype(F32)).astype(BF16)


def first_kernel(diag_ref, low_ref, inv_ref, high_ref, rest_ref, work):
    work[...] = diag_ref[...].astype(F32)
    low_ref[...] = jnp.zeros_like(low_ref)
    inv_ref[...] = jnp.zeros_like(inv_ref)
    factor_block(work, low_ref, inv_ref, 0, TILE)
    split_store(inv_ref, high_ref, rest_ref)


def second_kernel(side_ref, diag_ref, inv0_ref, low_ref, link_ref, high_ref, rest_ref, work, inv):
    low_ref[...] = jnp.zeros_like(low_ref)
    inv[...] = jnp.zeros_like(inv)
    for c in range(CAND):
        panel = dot_high(side_ref[c].astype(F32), inv0_ref[c], 1).astype(BF16)
        link_ref[c] = panel
        work[c] = diag_ref[c].astype(F32) - lax.dot_general(
            panel, panel, (((1,), (1,)), ((), ())), preferred_element_type=F32
        )
    factor_block(work, low_ref, inv, 0, TILE)
    split_store(inv, high_ref, rest_ref)


def whole(count):
    return [pl.BlockSpec(memory_space=pltpu.VMEM)] * count


def factor_first(diag):
    shape = diag.shape
    return pl.pallas_call(
        first_kernel,
        out_shape=[
            jax.ShapeDtypeStruct(shape, F32),
            jax.ShapeDtypeStruct(shape, F32),
            jax.ShapeDtypeStruct(shape, BF16),
            jax.ShapeDtypeStruct(shape, BF16),
        ],
        in_specs=whole(1),
        out_specs=whole(4),
        scratch_shapes=[pltpu.VMEM(shape, F32)],
        compiler_params=pltpu.CompilerParams(vmem_limit_bytes=40 * 2**20),
        cost_estimate=pl.CostEstimate(flops=20_000_000_000, bytes_accessed=8_000_000, transcendentals=0),
        name="factor_first",
    )(diag)


def factor_second(side, diag, inv0):
    shape = diag.shape
    return pl.pallas_call(
        second_kernel,
        out_shape=[
            jax.ShapeDtypeStruct(shape, F32),
            jax.ShapeDtypeStruct(shape, BF16),
            jax.ShapeDtypeStruct(shape, BF16),
            jax.ShapeDtypeStruct(shape, BF16),
        ],
        in_specs=whole(3),
        out_specs=whole(4),
        scratch_shapes=[pltpu.VMEM(shape, F32), pltpu.VMEM(shape, F32)],
        compiler_params=pltpu.CompilerParams(vmem_limit_bytes=40 * 2**20),
        cost_estimate=pl.CostEstimate(flops=20_000_000_000, bytes_accessed=8_000_000, transcendentals=0),
        name="factor_second",
    )(side, diag, inv0)


def mm(left, right, dims=(1, 0)):
    return lax.dot_general(
        left, right, (((dims[0],), (dims[1],)), ((), ())), preferred_element_type=F32
    )


def halves(value):
    high = value.astype(BF16)
    return high, (value - high.astype(F32)).astype(BF16)


def column_kernel(c0_ref, c1_ref, h0_ref, r0_ref, h1_ref, r1_ref, link_ref, out_ref):
    raw0 = c0_ref[0]
    panel0 = (mm(h0_ref[0], raw0) + mm(r0_ref[0], raw0)).astype(BF16)
    out_ref[0, :TILE, :] = panel0
    left1 = c1_ref[0].astype(F32) - mm(link_ref[0], panel0)
    high, rest = halves(left1)
    panel1 = mm(h1_ref[0], high) + mm(h1_ref[0], rest) + mm(r1_ref[0], high)
    out_ref[0, TILE:, :] = panel1.astype(BF16)


def column_panels(c0, c1, h0, r0, h1, r1, link):
    width = c0.shape[2]
    step = 512
    tall = pl.BlockSpec((1, TILE, TILE), lambda c, j: (c, 0, 0))
    wide = pl.BlockSpec((1, TILE, step), lambda c, j: (c, 0, j))
    return pl.pallas_call(
        column_kernel,
        grid=(CAND, width // step),
        out_shape=jax.ShapeDtypeStruct((CAND, 2 * TILE, width), BF16),
        in_specs=[wide, wide, tall, tall, tall, tall, tall],
        out_specs=pl.BlockSpec((1, 2 * TILE, step), lambda c, j: (c, 0, j)),
        compiler_params=pltpu.CompilerParams(vmem_limit_bytes=40 * 2**20),
        cost_estimate=pl.CostEstimate(flops=6_500_000_000, bytes_accessed=12_000_000, transcendentals=0),
        name="column_panels",
    )(c0, c1, h0, r0, h1, r1, link)


ROWS = 256


def final_kernel(
    place_ref, base_ref, rows0_ref, rows1_ref, cols_ref, low0_ref, low1_ref,
    h0_ref, r0_ref, h1_ref, r1_ref, link_ref, out_ref, left_ref,
):
    grid_row = place_ref[0]
    grid_column = place_ref[1]
    slot = pl.program_id(1)
    raw0 = rows0_ref[0]
    panel0 = mm(raw0, h0_ref[0], (1, 1)) + mm(raw0, r0_ref[0], (1, 1))
    round0 = panel0.astype(BF16)
    left1 = rows1_ref[0].astype(F32) - mm(round0, link_ref[0], (1, 1))
    high, rest = halves(left1)
    panel1 = mm(high, h1_ref[0], (1, 1)) + mm(rest, h1_ref[0], (1, 1)) + mm(high, r1_ref[0], (1, 1))
    round1 = panel1.astype(BF16)
    top = (slot == 0) & (grid_row < 2)
    update = mm(round0, cols_ref[0, :TILE, :]) + mm(round1, cols_ref[0, TILE:, :])
    value = jnp.where(top, 0.0, base_ref[0].astype(F32) - update)
    for j in range(8):
        out_ref[pl.ds(j, ROWS, stride=8), :] = value[:, 128 * j : 128 * (j + 1)]

    @pl.when(grid_column == 0)
    def _():
        first = jnp.where((slot == 0) & (grid_row == 0), low0_ref[0], panel0)
        for j in range(4):
            out_ref[pl.ds(j, ROWS, stride=8), :] = first[:, 128 * j : 128 * (j + 1)]

    @pl.when(grid_column == 1)
    def _():
        second = jnp.where((slot == 0) & (grid_row == 0), 0.0, panel1)
        second = jnp.where((slot == 0) & (grid_row == 1), low1_ref[0], second)
        for j in range(4):
            out_ref[pl.ds(j, ROWS, stride=8), :] = second[:, 128 * j : 128 * (j + 1)]


def final_update(place, base, rows0, rows1, cols, low0, low1, h0, r0, h1, r1, link):
    height = base.shape[1]
    slots = height // TILE
    per = TILE // ROWS
    block = lambda w: pl.BlockSpec((1, ROWS, w), lambda c, a, s: (c, a * per + s, 0))
    tall = pl.BlockSpec((1, TILE, TILE), lambda c, a, s: (c, 0, 0))
    low = pl.BlockSpec((1, ROWS, TILE), lambda c, a, s: (c, s, 0))
    out = pl.pallas_call(
        final_kernel,
        grid=(CAND, slots, per),
        out_shape=jax.ShapeDtypeStruct((CAND * height * 8, 128), F32),
        in_specs=[
            pl.BlockSpec(memory_space=pltpu.SMEM),
            block(2 * TILE),
            block(TILE),
            block(TILE),
            pl.BlockSpec((1, 2 * TILE, 2 * TILE), lambda c, a, s: (c, 0, 0)),
            low,
            low,
            tall, tall, tall, tall, tall,
        ],
        out_specs=pl.BlockSpec((ROWS * 8, 128), lambda c, a, s: ((c * slots + a) * per + s, 0)),
        scratch_shapes=[pltpu.VMEM((8, 128), F32)],
        compiler_params=pltpu.CompilerParams(vmem_limit_bytes=50 * 2**20),
        cost_estimate=pl.CostEstimate(flops=21_500_000_000, bytes_accessed=40_000_000, transcendentals=0),
        name="final_update",
    )(place, base, rows0, rows1, cols, low0, low1, h0, r0, h1, r1, link)
    return out


BOTH = ("prow", "pcol")
XS, ZS, YS = 4, 4, 4


def send(value, pairs):
    return lax.ppermute(value, BOTH, [(a[0] * 16 + a[1], b[0] * 16 + b[1]) for a, b in pairs])


def spread_tile(tile, cores):
    grid_column = lax.axis_index("pcol")
    grid_row = lax.axis_index("prow")
    x = grid_column % XS
    z = grid_column // XS
    y = grid_row // 2
    quarters = tile.reshape(CAND, XS, TILE // XS, TILE)
    mine = quarters[:, 0]
    for k in range(1, XS):
        got = send(quarters[:, k], [((c, 0), (c, k)) for c in cores])
        mine = jnp.where(x == k, got, mine)
    held = mine
    for k in range(1, ZS):
        got = send(mine, [((c, i), (c, k * XS + i)) for c in cores for i in range(XS)])
        held = jnp.where(z == k, got, held)
    mine = held
    for k in range(1, YS):
        got = send(mine, [((c, i), (k * 2 + c, i)) for c in cores for i in range(16)])
        held = jnp.where(y == k, got, held)
    parts = [held]
    for k in range(1, XS):
        parts.append(
            send(
                held,
                [
                    ((2 * j + c, w * XS + i), (2 * j + c, w * XS + (i + k) % XS))
                    for c in cores for j in range(YS) for w in range(ZS) for i in range(XS)
                ],
            )
        )
    turned = jnp.concatenate([parts[(XS - 1 - i) % XS] for i in range(2 * XS - 1)], 1)
    return lax.dynamic_slice_in_dim(turned, (XS - 1 - x) * (TILE // XS), TILE, axis=1)


def core_swap(value):
    return send(value, [((p, q), (p ^ 1, q)) for p in range(8) for q in range(16)])


def shards(covariance):
    height = 4 * TILE
    grid_row = lax.axis_index("prow")
    grid_column = lax.axis_index("pcol")
    core = grid_row % 2
    base = covariance.reshape(CAND, height, 2 * TILE)
    corner = covariance[:, 0, 0, :, 0, 0, :]

    got = spread_tile(corner, (0,))
    swapped = core_swap(got)
    diag0 = jnp.where(core == 0, got, swapped)
    moved = send(corner, [((1, 1), (0, 0))])
    second = jnp.where((grid_row == 0) & (grid_column == 0), moved, corner)
    got = spread_tile(second, (0, 1))
    swapped = core_swap(got)
    diag1 = jnp.where(core == 0, got, swapped)
    side = jnp.where(core == 0, swapped, got)

    column = covariance[:, :, 0, :, 0, 0, :].reshape(CAND, 16, height // 16, TILE)
    held0 = column[:, 0]
    held1 = column[:, 1]
    for k in range(2, 16):
        j = k + 1 if k < 15 else 2
        piece = jnp.where(grid_column == 0, column[:, k], column[:, j])
        got = lax.ppermute(piece, "pcol", [(0, k), (1, j)])
        held0 = jnp.where(grid_column == k, got, held0)
        held1 = jnp.where(grid_column == j, got, held1)
    piece = jnp.where(grid_column == 0, column[:, 1], column[:, 0])
    got = lax.ppermute(piece, "pcol", [(0, 1), (1, 0)])
    held0 = jnp.where(grid_column == 1, got, held0)
    held1 = jnp.where(grid_column == 0, got, held1)
    rows0 = lax.all_gather(held0, "pcol", axis=1).reshape(CAND, height, TILE)
    rows1 = lax.all_gather(held1, "pcol", axis=1).reshape(CAND, height, TILE)

    wide = covariance[:, 0, 0].reshape(CAND, TILE, 2 * TILE)
    y = grid_row // 2
    shift = lambda d: [((c, q), (2 * d + c, q)) for c in range(2) for q in range(16)]
    up = send(wide, shift(1))
    down = send(wide, shift(3))
    mine = jnp.where(y == 1, up, jnp.where(y == 3, down, wide))
    left = send(mine[:, :, :TILE], [((2 + c, q), (4 + c, q)) for c in range(2) for q in range(16)])
    right = send(mine[:, :, TILE:], [((6 + c, q), (4 + c, q)) for c in range(2) for q in range(16)])
    mine = jnp.where(y == 2, jnp.concatenate([left, right], 2), mine)
    other = core_swap(mine)
    cols0 = jnp.where(core == 0, mine, other)
    cols1 = jnp.where(core == 0, other, mine)

    low0, inv0, h0, r0 = factor_first(diag0)
    low1, link, h1, r1 = factor_second(side, diag1, inv0)
    cols = column_panels(cols0, cols1, h0, r0, h1, r1, link)
    place = jnp.stack([grid_row, grid_column]).astype(jnp.int32)
    out = final_update(place, base, rows0, rows1, cols, low0, low1, h0, r0, h1, r1, link)
    return out.reshape(covariance.shape)


def solution(mesh):
    spec = P(None, None, "prow", None, None, "pcol", None)
    return jax.shard_map(shards, mesh=mesh, in_specs=(spec,), out_specs=spec, check_vma=False)
```

```python
import jax
import jax.numpy as jnp
from jax import lax
from jax.experimental import pallas as pl
from jax.experimental.pallas import tpu as pltpu
from jax.sharding import PartitionSpec as P

TILE = 512
CAND = 2
BASE = 64
F32 = jnp.float32
BF16 = jnp.bfloat16


def lane_pick(value, column):
    lane = lax.broadcasted_iota(jnp.int32, (8, 128), 1)
    index = jnp.where(lane < BASE, column, BASE + column)
    return jnp.take_along_axis(value, index, axis=1, mode="promise_in_bounds")


def row_spread(value, row):
    return jnp.broadcast_to(value[row : row + 1, :], (8, 128))


def factor_base(groups):
    lane = lax.broadcasted_iota(jnp.int32, (8, 128), 1)
    half = jnp.where(lane < BASE, lane, lane - BASE)
    sub = lax.broadcasted_iota(jnp.int32, (8, 128), 0)
    work = list(groups)
    inverse = [jnp.where(half == sub + 8 * i, 1.0, 0.0).astype(F32) for i in range(8)]
    lower = [jnp.zeros((8, 128), F32) for _ in range(8)]
    for i in range(8):
        rows = [row_spread(work[i], j) for j in range(8)]
        inv_rows = [row_spread(inverse[i], j) for j in range(8)]
        entry = [
            [lane_pick(rows[j], 8 * i + m) if m >= j else None for m in range(8)] for j in range(8)
        ]
        factor = [[None] * 8 for _ in range(8)]
        scale = [None] * 8
        for j in range(8):
            scale[j] = lax.rsqrt(entry[j][j])
            for m in range(j + 1, 8):
                factor[m][j] = entry[j][m] * scale[j]
            for a in range(j + 1, 8):
                for b in range(a, 8):
                    entry[a][b] = entry[a][b] - factor[a][j] * factor[b][j]
            rows[j] = rows[j] * scale[j]
            inv_rows[j] = inv_rows[j] * scale[j]
            for m in range(j + 1, 8):
                rows[m] = rows[m] - factor[m][j] * rows[j]
                inv_rows[m] = inv_rows[m] - factor[m][j] * inv_rows[j]
        merged = inv_rows[0]
        for j in range(1, 8):
            merged = jnp.where(sub == j, inv_rows[j], merged)
        inverse[i] = merged
        for q in range(i, 8):
            column = [lane_pick(work[q], 8 * i + j) for j in range(8)]
            for j in range(8):
                column[j] = column[j] * scale[j]
                for m in range(j + 1, 8):
                    column[m] = column[m] - column[j] * factor[m][j]
                here = half == 8 * i + j
                if q == i:
                    here = here & (sub >= j)
                lower[q] = jnp.where(here, column[j], lower[q])
            if q > i:
                for j in range(8):
                    work[q] = work[q] - column[j] * rows[j]
                    inverse[q] = inverse[q] - column[j] * inv_rows[j]
    return lower, inverse


def dot_high(left, right, right_dim):
    return lax.dot_general(
        left,
        right,
        (((1,), (right_dim,)), ((), ())),
        precision=lax.Precision.HIGHEST,
        preferred_element_type=F32,
    )


def factor_block(work, low, inv, start, size):
    if size == BASE:
        window = start // 128 * 128
        odd = start % 128 != 0
        rows = slice(start, start + BASE)
        lane = lax.broadcasted_iota(jnp.int32, (BASE, 128), 1)
        first = work[0, rows, window : window + 128]
        second = work[1, rows, window : window + 128]
        if odd:
            first = pltpu.roll(first, BASE, 1)
        else:
            second = pltpu.roll(second, BASE, 1)
        both = jnp.where(lane < BASE, first, second)
        lower, inverse = factor_base([both[8 * i : 8 * i + 8, :] for i in range(8)])
        for target, parts in ((low, lower), (inv, inverse)):
            value = jnp.concatenate(parts, 0)
            rolled = pltpu.roll(value, BASE, 1)
            cols = slice(start, start + BASE)
            if odd:
                target[0, rows, cols] = rolled[:, BASE:]
                target[1, rows, cols] = value[:, BASE:]
            else:
                target[0, rows, cols] = value[:, :BASE]
                target[1, rows, cols] = rolled[:, :BASE]
        return
    half = size // 2
    top = slice(start, start + half)
    bottom = slice(start + half, start + size)
    factor_block(work, low, inv, start, half)
    for c in range(CAND):
        below = dot_high(work[c, bottom, top], inv[c, top, top], 1)
        low[c, bottom, top] = below
        work[c, bottom, bottom] = work[c, bottom, bottom] - dot_high(below, below, 1)
    factor_block(work, low, inv, start + half, half)
    for c in range(CAND):
        inner = dot_high(low[c, bottom, top], inv[c, top, top], 0)
        inv[c, bottom, top] = -dot_high(inv[c, bottom, bottom], inner, 0)


def split_store(inv, high_ref, rest_ref):
    for c in range(CAND):
        value = inv[c]
        high = value.astype(BF16)
        high_ref[c] = high
        rest_ref[c] = (value - high.astype(F32)).astype(BF16)


def unpack_lower(work, packed):
    half = TILE // 2
    for c in range(CAND):
        work[c, :half, :half] = packed[c, :half].astype(F32)
        work[c, half:, :half] = packed[c, half : 2 * half].astype(F32)
        work[c, half:, half:] = packed[c, 2 * half : 3 * half].astype(F32)


def sort_parts(place_ref, own_ref, other_ref, first, second, offset):
    step = own_ref.shape[2]
    odd = lax.rem(place_ref[0], 2)
    for k in range(4):
        start = lax.rem(place_ref[2] + 4 - k, 4) * step
        low = pl.ds(pl.multiple_of(start, 16), step)
        high = pl.ds(pl.multiple_of(start + offset, 16), step)

        @pl.when(odd == 0)
        def _():
            first[:, low, :] = own_ref[k]
            second[:, high, :] = other_ref[k]

        @pl.when(odd == 1)
        def _():
            first[:, low, :] = other_ref[k]
            second[:, high, :] = own_ref[k]


def first_kernel(
    place_ref, own_ref, other_ref, low_ref, inv_ref, high_ref, rest_ref, packed, work
):
    sort_parts(place_ref, own_ref, other_ref, packed, packed, 3 * TILE // 4)
    unpack_lower(work, packed)
    low_ref[...] = jnp.zeros_like(low_ref)
    inv_ref[...] = jnp.zeros_like(inv_ref)
    factor_block(work, low_ref, inv_ref, 0, TILE)
    split_store(inv_ref, high_ref, rest_ref)


def second_kernel(
    place_ref, own_ref, other_ref, inv0_ref, low_ref, link_ref, high_ref, rest_ref,
    diag, side, work, inv,
):
    low_ref[...] = jnp.zeros_like(low_ref)
    inv[...] = jnp.zeros_like(inv)
    sort_parts(place_ref, own_ref, other_ref, diag, side, 0)
    unpack_lower(work, diag)
    half = TILE // 2
    for c in range(CAND):
        panel = (
            dot_high(side[c, :TILE].astype(F32), inv0_ref[c, :, :half], 1)
            + dot_high(side[c, TILE:].astype(F32), inv0_ref[c, :, half:], 1)
        ).astype(BF16)
        link_ref[c] = panel
        work[c] = work[c] - lax.dot_general(
            panel, panel, (((1,), (1,)), ((), ())), preferred_element_type=F32
        )
    factor_block(work, low_ref, inv, 0, TILE)
    split_store(inv, high_ref, rest_ref)


def whole(count):
    return [pl.BlockSpec(memory_space=pltpu.VMEM)] * count


def factor_first(place, own, other):
    shape = (CAND, TILE, TILE)
    return pl.pallas_call(
        first_kernel,
        out_shape=[
            jax.ShapeDtypeStruct(shape, F32),
            jax.ShapeDtypeStruct(shape, F32),
            jax.ShapeDtypeStruct(shape, BF16),
            jax.ShapeDtypeStruct(shape, BF16),
        ],
        in_specs=[pl.BlockSpec(memory_space=pltpu.SMEM)] + whole(2),
        out_specs=whole(4),
        scratch_shapes=[
            pltpu.VMEM((CAND, 3 * TILE // 2, TILE // 2), BF16),
            pltpu.VMEM(shape, F32),
        ],
        compiler_params=pltpu.CompilerParams(vmem_limit_bytes=40 * 2**20),
        cost_estimate=pl.CostEstimate(flops=20_000_000_000, bytes_accessed=8_000_000, transcendentals=0),
        name="factor_first",
    )(place, own, other)


def factor_second(place, own, other, inv0):
    shape = (CAND, TILE, TILE)
    return pl.pallas_call(
        second_kernel,
        out_shape=[
            jax.ShapeDtypeStruct(shape, F32),
            jax.ShapeDtypeStruct(shape, BF16),
            jax.ShapeDtypeStruct(shape, BF16),
            jax.ShapeDtypeStruct(shape, BF16),
        ],
        in_specs=[pl.BlockSpec(memory_space=pltpu.SMEM)] + whole(3),
        out_specs=whole(4),
        scratch_shapes=[
            pltpu.VMEM((CAND, 2 * TILE, TILE // 2), BF16),
            pltpu.VMEM((CAND, 2 * TILE, TILE // 2), BF16),
            pltpu.VMEM(shape, F32),
            pltpu.VMEM(shape, F32),
        ],
        compiler_params=pltpu.CompilerParams(vmem_limit_bytes=40 * 2**20),
        cost_estimate=pl.CostEstimate(flops=20_000_000_000, bytes_accessed=8_000_000, transcendentals=0),
        name="factor_second",
    )(place, own, other, inv0)


def mm(left, right, dims=(1, 0)):
    return lax.dot_general(
        left, right, (((dims[0],), (dims[1],)), ((), ())), preferred_element_type=F32
    )


def halves(value):
    high = value.astype(BF16)
    return high, (value - high.astype(F32)).astype(BF16)


def column_kernel(c0_ref, c1_ref, h0_ref, r0_ref, h1_ref, r1_ref, link_ref, out_ref):
    raw0 = c0_ref[0]
    panel0 = (mm(h0_ref[0], raw0) + mm(r0_ref[0], raw0)).astype(BF16)
    out_ref[0, :TILE, :] = panel0
    left1 = c1_ref[0].astype(F32) - mm(link_ref[0], panel0)
    high, rest = halves(left1)
    panel1 = mm(h1_ref[0], high) + mm(h1_ref[0], rest) + mm(r1_ref[0], high)
    out_ref[0, TILE:, :] = panel1.astype(BF16)


def column_panels(c0, c1, h0, r0, h1, r1, link):
    width = c0.shape[2]
    step = 512
    tall = pl.BlockSpec((1, TILE, TILE), lambda c, j: (c, 0, 0))
    wide = pl.BlockSpec((1, TILE, step), lambda c, j: (c, 0, j))
    return pl.pallas_call(
        column_kernel,
        grid=(CAND, width // step),
        out_shape=jax.ShapeDtypeStruct((CAND, 2 * TILE, width), BF16),
        in_specs=[wide, wide, tall, tall, tall, tall, tall],
        out_specs=pl.BlockSpec((1, 2 * TILE, step), lambda c, j: (c, 0, j)),
        compiler_params=pltpu.CompilerParams(vmem_limit_bytes=40 * 2**20),
        cost_estimate=pl.CostEstimate(flops=6_500_000_000, bytes_accessed=12_000_000, transcendentals=0),
        name="column_panels",
    )(c0, c1, h0, r0, h1, r1, link)


ROWS = 256


def final_kernel(
    place_ref, base_ref, rows_ref, cols_ref, low0_ref, low1_ref,
    h0_ref, r0_ref, h1_ref, r1_ref, link_ref, out_ref, left_ref,
):
    grid_row = place_ref[0]
    grid_column = place_ref[1]
    slot = pl.program_id(1)
    raw0 = rows_ref[:, 0, 0].reshape(ROWS, TILE)
    panel0 = mm(raw0, h0_ref[0], (1, 1)) + mm(raw0, r0_ref[0], (1, 1))
    round0 = panel0.astype(BF16)
    left1 = rows_ref[:, 1, 0].reshape(ROWS, TILE).astype(F32) - mm(round0, link_ref[0], (1, 1))
    high, rest = halves(left1)
    panel1 = mm(high, h1_ref[0], (1, 1)) + mm(rest, h1_ref[0], (1, 1)) + mm(high, r1_ref[0], (1, 1))
    round1 = panel1.astype(BF16)
    top = (slot == 0) & (grid_row < 2)
    update = mm(round0, cols_ref[0, :TILE, :]) + mm(round1, cols_ref[0, TILE:, :])
    value = jnp.where(top, 0.0, base_ref[0].astype(F32) - update)
    for j in range(8):
        out_ref[pl.ds(j, ROWS, stride=8), :] = value[:, 128 * j : 128 * (j + 1)]

    @pl.when(grid_column == 0)
    def _():
        first = jnp.where((slot == 0) & (grid_row == 0), low0_ref[0], panel0)
        for j in range(4):
            out_ref[pl.ds(j, ROWS, stride=8), :] = first[:, 128 * j : 128 * (j + 1)]

    @pl.when(grid_column == 1)
    def _():
        second = jnp.where((slot == 0) & (grid_row == 0), 0.0, panel1)
        second = jnp.where((slot == 0) & (grid_row == 1), low1_ref[0], second)
        for j in range(4):
            out_ref[pl.ds(j, ROWS, stride=8), :] = second[:, 128 * j : 128 * (j + 1)]


def final_update(place, base, rows, cols, low0, low1, h0, r0, h1, r1, link):
    height = base.shape[1]
    slots = height // TILE
    per = TILE // ROWS
    block = lambda w: pl.BlockSpec((1, ROWS, w), lambda c, a, s: (c, a * per + s, 0))
    tall = pl.BlockSpec((1, TILE, TILE), lambda c, a, s: (c, 0, 0))
    low = pl.BlockSpec((1, ROWS, TILE), lambda c, a, s: (c, s, 0))
    out = pl.pallas_call(
        final_kernel,
        grid=(CAND, slots, per),
        out_shape=jax.ShapeDtypeStruct((CAND * height * 8, 128), F32),
        in_specs=[
            pl.BlockSpec(memory_space=pltpu.SMEM),
            block(2 * TILE),
            pl.BlockSpec((ROWS // 128, 2, 1, 128, TILE), lambda c, a, s: (a * per + s, 0, c, 0, 0)),
            pl.BlockSpec((1, 2 * TILE, 2 * TILE), lambda c, a, s: (c, 0, 0)),
            low,
            low,
            tall, tall, tall, tall, tall,
        ],
        out_specs=pl.BlockSpec((ROWS * 8, 128), lambda c, a, s: ((c * slots + a) * per + s, 0)),
        scratch_shapes=[pltpu.VMEM((8, 128), F32)],
        compiler_params=pltpu.CompilerParams(vmem_limit_bytes=50 * 2**20),
        cost_estimate=pl.CostEstimate(flops=21_500_000_000, bytes_accessed=40_000_000, transcendentals=0),
        name="final_update",
    )(place, base, rows, cols, low0, low1, h0, r0, h1, r1, link)
    return out


BOTH = ("prow", "pcol")
XS, ZS, YS = 4, 4, 4


def send(value, pairs):
    return lax.ppermute(value, BOTH, [(a[0] * 16 + a[1], b[0] * 16 + b[1]) for a, b in pairs])


def after(value, *earlier):
    return lax.optimization_barrier((value,) + earlier)[0]


def around_x(piece):
    return [
        send(
            piece,
            [
                ((p, w * XS + i), (p, w * XS + (i + k) % XS))
                for p in range(8) for w in range(ZS) for i in range(XS)
            ],
        )
        for k in range(1, XS)
    ]


def ring_spread(value, position, core, place, *gate):
    def pairs(core_index, source, target):
        return [
            ((a[0] * 2 + core_index, a[1]), (b[0] * 2 + core_index, b[1]))
            for a, b in zip(place(source), place(target))
        ]

    got = send(value, pairs(0, 0, 1) + pairs(1, 0, 3))
    value = jnp.where(position == jnp.where(core == 0, 1, 3), got, value)
    if gate:
        value = after(value, *gate)
    got = send(value, pairs(0, 0, 3) + pairs(0, 1, 2) + pairs(1, 0, 1) + pairs(1, 3, 2))
    last = (position == 2) | (position == jnp.where(core == 0, 3, 1))
    return jnp.where(last, got, value)


def chip(z, x):
    return z % ZS * XS + x % XS


def scatter_plan(s):
    east = [chip(0, s + 1), chip(1, s + 1), chip(3, s + 1), chip(2, s + 1)]
    west = [chip(0, s - 1), chip(1, s - 1), chip(3, s - 1), chip(2, s - 1)]
    north = [chip(1, s), chip(2, s), chip(1, s + 2), chip(2, s + 2)]
    south = [chip(3, s), None, chip(3, s + 2), chip(0, s + 2)]
    return [east, west, north, south]


def core_swap(value):
    return send(value, [((p, q), (p ^ 1, q)) for p in range(8) for q in range(16)])


def shards(covariance):
    height = 4 * TILE
    grid_row = lax.axis_index("prow")
    grid_column = lax.axis_index("pcol")
    core = grid_row % 2
    x = grid_column % XS
    z = grid_column // XS
    y = grid_row // 2
    half = TILE // 2
    place = jnp.stack([grid_row, grid_column, x]).astype(jnp.int32)

    corner = covariance[:, 0, 0, :, 0, 0, :]
    lower = jnp.concatenate(
        [corner[:, :half, :half], corner[:, half:, :half], corner[:, half:, half:]], 1
    )
    share = 3 * TILE // 4
    halved = send(lower[:, share:], [((0, 0), (1, 0))])
    moved = send(lower, [((1, 1), (0, 0))])
    first = jnp.where(core == 0, lower[:, :share], halved)
    second = jnp.where(
        core == 0,
        jnp.concatenate([moved, lower[:, :half]], 1),
        jnp.concatenate([corner[:, :, :half], corner[:, :, half:]], 1),
    )

    def quarter(k):
        return jnp.concatenate(
            [
                first[:, k * share // XS : (k + 1) * share // XS],
                second[:, k * half : (k + 1) * half],
            ],
            1,
        )

    held = quarter(0)
    dealt = [send(quarter(k), [((c, 0), (c, k)) for c in range(2)]) for k in range(1, XS)]
    for k in range(1, XS):
        held = jnp.where(x == k, dealt[k - 1], held)

    pieces = covariance[:, :, 0, :, 0, 0, :].reshape(CAND, 16, height // 16, TILE)
    plans = [scatter_plan(0), scatter_plan(1)]
    level1 = []
    for g in range(4):
        def message(s):
            members = [plans[s][g][0] if m is None else m for m in plans[s][g]]
            return jnp.stack([pieces[:, m] for m in members])
        value = jnp.where(grid_column == 0, message(0), message(1))
        if g < 2:
            value = after(value, *dealt)
        level1.append(
            lax.ppermute(value, "pcol", [(s, plans[s][g][0]) for s in range(2)])
        )

    held = ring_spread(
        held, z, core, lambda i: [(0, i * XS + j) for j in range(XS)]
    )
    group_gate = held
    held = ring_spread(
        held, y, core, lambda i: [(i, q) for q in range(16)]
    )

    holding = [[plans[s][g][0] for g in range(4)] for s in range(2)]
    level1 = list(lax.optimization_barrier((*level1, group_gate)))[:4]
    group = level1[3]
    for g in range(3):
        mine = (grid_column == holding[0][g]) | (grid_column == holding[1][g])
        group = jnp.where(mine, level1[g], group)
    rank1 = grid_column == holding[1][0]
    for g in range(1, 4):
        rank1 = rank1 | (grid_column == holding[1][g])
    turns = [(1, 1), (2, 3), (3, 2)]
    level2 = []
    for i0, i1 in turns:
        value = jnp.where(rank1, group[i1], group[i0])
        pairs = [
            (plans[s][g][0], plans[s][g][i])
            for s, i in ((0, i0), (1, i1)) for g in range(4) if plans[s][g][i] is not None
        ]
        level2.append(lax.ppermute(value, "pcol", pairs))
    level2 = list(lax.optimization_barrier((*level2, held)))[:3]
    own = [pieces[:, 0], pieces[:, 1]]
    rows_held = []
    for s in range(2):
        value = own[s]
        for g in range(4):
            value = jnp.where(grid_column == plans[s][g][0], group[0], value)
            for n, turn in enumerate(turns):
                target = plans[s][g][turn[s]]
                if target is not None:
                    value = jnp.where(grid_column == target, level2[n], value)
        rows_held.append(value)
    rows = lax.all_gather(jnp.stack(rows_held), "pcol", axis=0)

    around0 = around_x(held[:, : share // XS])
    own0 = jnp.stack([held[:, : share // XS]] + around0)
    other0 = core_swap(own0)
    later = after(held, other0)[:, share // XS :]
    around1 = around_x(later)

    wide = covariance[:, 0, 0].reshape(CAND, TILE, 2 * TILE)
    mine = ring_spread(
        after(wide, group_gate), y, core, lambda i: [(i, q) for q in range(16)], *around0
    )

    low0, inv0, h0, r0 = factor_first(place, own0, other0)
    own1 = jnp.stack(lax.optimization_barrier((later, *around1, h0))[:4])
    other1 = core_swap(own1)
    mine = after(mine, h0)
    other = core_swap(mine)
    cols0 = jnp.where(core == 0, mine, other)
    cols1 = jnp.where(core == 0, other, mine)
    low1, link, h1, r1 = factor_second(place, own1, other1, inv0)
    cols = column_panels(cols0, cols1, h0, r0, h1, r1, link)
    base = after(covariance, cols).reshape(CAND, height, 2 * TILE)
    out = final_update(place, base, rows, cols, low0, low1, h0, r0, h1, r1, link)
    return out.reshape(covariance.shape)


def solution(mesh):
    spec = P(None, None, "prow", None, None, "pcol", None)
    return jax.shard_map(shards, mesh=mesh, in_specs=(spec,), out_specs=spec, check_vma=False)
```

```python
import jax
import jax.numpy as jnp
from jax import lax
from jax.experimental import pallas as pl
from jax.experimental.pallas import tpu as pltpu
from jax.sharding import PartitionSpec as P

TILE = 512
CAND = 2
BASE = 64
F32 = jnp.float32
BF16 = jnp.bfloat16


def lane_pick(value, column):
    lane = lax.broadcasted_iota(jnp.int32, (8, 128), 1)
    index = jnp.where(lane < BASE, column, BASE + column)
    return jnp.take_along_axis(value, index, axis=1, mode="promise_in_bounds")


def row_spread(value, row):
    return jnp.broadcast_to(value[row : row + 1, :], (8, 128))


def factor_base(groups):
    lane = lax.broadcasted_iota(jnp.int32, (8, 128), 1)
    half = jnp.where(lane < BASE, lane, lane - BASE)
    sub = lax.broadcasted_iota(jnp.int32, (8, 128), 0)
    work = list(groups)
    inverse = [jnp.where(half == sub + 8 * i, 1.0, 0.0).astype(F32) for i in range(8)]
    lower = [jnp.zeros((8, 128), F32) for _ in range(8)]
    for i in range(8):
        rows = [row_spread(work[i], j) for j in range(8)]
        inv_rows = [row_spread(inverse[i], j) for j in range(8)]
        entry = [
            [lane_pick(rows[j], 8 * i + m) if m >= j else None for m in range(8)] for j in range(8)
        ]
        factor = [[None] * 8 for _ in range(8)]
        scale = [None] * 8
        for j in range(8):
            scale[j] = lax.rsqrt(entry[j][j])
            for m in range(j + 1, 8):
                factor[m][j] = entry[j][m] * scale[j]
            for a in range(j + 1, 8):
                for b in range(a, 8):
                    entry[a][b] = entry[a][b] - factor[a][j] * factor[b][j]
            rows[j] = rows[j] * scale[j]
            inv_rows[j] = inv_rows[j] * scale[j]
            for m in range(j + 1, 8):
                rows[m] = rows[m] - factor[m][j] * rows[j]
                inv_rows[m] = inv_rows[m] - factor[m][j] * inv_rows[j]
        merged = inv_rows[0]
        for j in range(1, 8):
            merged = jnp.where(sub == j, inv_rows[j], merged)
        inverse[i] = merged
        for q in range(i, 8):
            column = [lane_pick(work[q], 8 * i + j) for j in range(8)]
            for j in range(8):
                column[j] = column[j] * scale[j]
                for m in range(j + 1, 8):
                    column[m] = column[m] - column[j] * factor[m][j]
                here = half == 8 * i + j
                if q == i:
                    here = here & (sub >= j)
                lower[q] = jnp.where(here, column[j], lower[q])
            if q > i:
                for j in range(8):
                    work[q] = work[q] - column[j] * rows[j]
                    inverse[q] = inverse[q] - column[j] * inv_rows[j]
    return lower, inverse


def dot_high(left, right, right_dim):
    return lax.dot_general(
        left,
        right,
        (((1,), (right_dim,)), ((), ())),
        precision=lax.Precision.HIGHEST,
        preferred_element_type=F32,
    )


def factor_bottom(work, low, inv, start, size):
    half = size // 2
    top = slice(start, start + half)
    bottom = slice(start + half, start + size)
    factor_block(work, low, inv, start + half, half)
    for c in range(CAND):
        inner = dot_high(low[c, bottom, top], inv[c, top, top], 0)
        inv[c, bottom, top] = -dot_high(inv[c, bottom, bottom], inner, 0)


def factor_top(work, low, inv, start, size):
    half = size // 2
    top = slice(start, start + half)
    bottom = slice(start + half, start + size)
    factor_block(work, low, inv, start, half)
    for c in range(CAND):
        below = dot_high(work[c, bottom, top], inv[c, top, top], 1)
        low[c, bottom, top] = below
        work[c, bottom, bottom] = work[c, bottom, bottom] - dot_high(below, below, 1)


def factor_block(work, low, inv, start, size):
    if size == BASE:
        window = start // 128 * 128
        odd = start % 128 != 0
        rows = slice(start, start + BASE)
        lane = lax.broadcasted_iota(jnp.int32, (BASE, 128), 1)
        first = work[0, rows, window : window + 128]
        second = work[1, rows, window : window + 128]
        if odd:
            first = pltpu.roll(first, BASE, 1)
        else:
            second = pltpu.roll(second, BASE, 1)
        both = jnp.where(lane < BASE, first, second)
        lower, inverse = factor_base([both[8 * i : 8 * i + 8, :] for i in range(8)])
        for target, parts in ((low, lower), (inv, inverse)):
            value = jnp.concatenate(parts, 0)
            rolled = pltpu.roll(value, BASE, 1)
            cols = slice(start, start + BASE)
            if odd:
                target[0, rows, cols] = rolled[:, BASE:]
                target[1, rows, cols] = value[:, BASE:]
            else:
                target[0, rows, cols] = value[:, :BASE]
                target[1, rows, cols] = rolled[:, :BASE]
        return
    factor_top(work, low, inv, start, size)
    factor_bottom(work, low, inv, start, size)


def split_store(inv, high_ref, rest_ref):
    for c in range(CAND):
        value = inv[c]
        high = value.astype(BF16)
        high_ref[c] = high
        rest_ref[c] = (value - high.astype(F32)).astype(BF16)


def unpack_lower(work, packed):
    half = TILE // 2
    for c in range(CAND):
        work[c, :half, :half] = packed[c, :half].astype(F32)
        work[c, half:, :half] = packed[c, half : 2 * half].astype(F32)
        work[c, half:, half:] = packed[c, 2 * half : 3 * half].astype(F32)


def sort_parts(place_ref, own_ref, other_ref, first, second, offset):
    step = own_ref.shape[2]
    odd = lax.rem(place_ref[0], 2)
    for k in range(4):
        start = lax.rem(place_ref[2] + 4 - k, 4) * step
        low = pl.ds(pl.multiple_of(start, 16), step)
        high = pl.ds(pl.multiple_of(start + offset, 16), step)

        @pl.when(odd == 0)
        def _():
            first[:, low, :] = own_ref[k]
            second[:, high, :] = other_ref[k]

        @pl.when(odd == 1)
        def _():
            first[:, low, :] = other_ref[k]
            second[:, high, :] = own_ref[k]


def first_kernel(place_ref, own_ref, other_ref, low_ref, inv_ref, work, packed):
    sort_parts(place_ref, own_ref, other_ref, packed, packed, 3 * TILE // 4)
    unpack_lower(work, packed)
    low_ref[...] = jnp.zeros_like(low_ref)
    inv_ref[...] = jnp.zeros_like(inv_ref)
    factor_top(work, low_ref, inv_ref, 0, TILE)


def rest_kernel(
    low_in, inv_in, work_in, low_ref, inv_ref, high_ref, rest_ref, work
):
    low_ref[...] = low_in[...]
    inv_ref[...] = inv_in[...]
    work[...] = work_in[...]
    factor_bottom(work, low_ref, inv_ref, 0, TILE)
    split_store(inv_ref, high_ref, rest_ref)


def second_kernel(
    place_ref, own_ref, other_ref, inv0_ref, low_ref, inv_ref, work, link_ref, diag, side
):
    low_ref[...] = jnp.zeros_like(low_ref)
    inv_ref[...] = jnp.zeros_like(inv_ref)
    sort_parts(place_ref, own_ref, other_ref, diag, side, 0)
    unpack_lower(work, diag)
    half = TILE // 2
    for c in range(CAND):
        panel = (
            dot_high(side[c, :TILE].astype(F32), inv0_ref[c, :, :half], 1)
            + dot_high(side[c, TILE:].astype(F32), inv0_ref[c, :, half:], 1)
        ).astype(BF16)
        link_ref[c] = panel
        work[c] = work[c] - lax.dot_general(
            panel, panel, (((1,), (1,)), ((), ())), preferred_element_type=F32
        )
    factor_top(work, low_ref, inv_ref, 0, TILE)


def whole(count):
    return [pl.BlockSpec(memory_space=pltpu.VMEM)] * count


def factor_first(place, own, other):
    shape = (CAND, TILE, TILE)
    return pl.pallas_call(
        first_kernel,
        out_shape=[jax.ShapeDtypeStruct(shape, F32)] * 3,
        in_specs=[pl.BlockSpec(memory_space=pltpu.SMEM)] + whole(2),
        out_specs=whole(3),
        scratch_shapes=[pltpu.VMEM((CAND, 3 * TILE // 2, TILE // 2), BF16)],
        compiler_params=pltpu.CompilerParams(vmem_limit_bytes=40 * 2**20),
        cost_estimate=pl.CostEstimate(flops=10_000_000_000, bytes_accessed=8_000_000, transcendentals=0),
        name="factor_first",
    )(place, own, other)


def factor_rest(low, inv, work):
    shape = (CAND, TILE, TILE)
    return pl.pallas_call(
        rest_kernel,
        out_shape=[
            jax.ShapeDtypeStruct(shape, F32),
            jax.ShapeDtypeStruct(shape, F32),
            jax.ShapeDtypeStruct(shape, BF16),
            jax.ShapeDtypeStruct(shape, BF16),
        ],
        in_specs=whole(3),
        out_specs=whole(4),
        scratch_shapes=[pltpu.VMEM(shape, F32)],
        compiler_params=pltpu.CompilerParams(vmem_limit_bytes=40 * 2**20),
        cost_estimate=pl.CostEstimate(flops=10_000_000_000, bytes_accessed=8_000_000, transcendentals=0),
        name="factor_rest",
    )(low, inv, work)


def factor_second(place, own, other, inv0):
    shape = (CAND, TILE, TILE)
    return pl.pallas_call(
        second_kernel,
        out_shape=[jax.ShapeDtypeStruct(shape, F32)] * 3 + [jax.ShapeDtypeStruct(shape, BF16)],
        in_specs=[pl.BlockSpec(memory_space=pltpu.SMEM)] + whole(3),
        out_specs=whole(4),
        scratch_shapes=[
            pltpu.VMEM((CAND, 2 * TILE, TILE // 2), BF16),
            pltpu.VMEM((CAND, 2 * TILE, TILE // 2), BF16),
        ],
        compiler_params=pltpu.CompilerParams(vmem_limit_bytes=40 * 2**20),
        cost_estimate=pl.CostEstimate(flops=10_000_000_000, bytes_accessed=8_000_000, transcendentals=0),
        name="factor_second",
    )(place, own, other, inv0)


def mm(left, right, dims=(1, 0)):
    return lax.dot_general(
        left, right, (((dims[0],), (dims[1],)), ((), ())), preferred_element_type=F32
    )


def halves(value):
    high = value.astype(BF16)
    return high, (value - high.astype(F32)).astype(BF16)


def column_kernel(c0_ref, c1_ref, h0_ref, r0_ref, h1_ref, r1_ref, link_ref, out_ref):
    raw0 = c0_ref[0]
    panel0 = (mm(h0_ref[0], raw0) + mm(r0_ref[0], raw0)).astype(BF16)
    out_ref[0, :TILE, :] = panel0
    left1 = c1_ref[0].astype(F32) - mm(link_ref[0], panel0)
    high, rest = halves(left1)
    panel1 = mm(h1_ref[0], high) + mm(h1_ref[0], rest) + mm(r1_ref[0], high)
    out_ref[0, TILE:, :] = panel1.astype(BF16)


def column_panels(c0, c1, h0, r0, h1, r1, link):
    width = c0.shape[2]
    step = 512
    tall = pl.BlockSpec((1, TILE, TILE), lambda c, j: (c, 0, 0))
    wide = pl.BlockSpec((1, TILE, step), lambda c, j: (c, 0, j))
    return pl.pallas_call(
        column_kernel,
        grid=(CAND, width // step),
        out_shape=jax.ShapeDtypeStruct((CAND, 2 * TILE, width), BF16),
        in_specs=[wide, wide, tall, tall, tall, tall, tall],
        out_specs=pl.BlockSpec((1, 2 * TILE, step), lambda c, j: (c, 0, j)),
        compiler_params=pltpu.CompilerParams(vmem_limit_bytes=40 * 2**20),
        cost_estimate=pl.CostEstimate(flops=6_500_000_000, bytes_accessed=12_000_000, transcendentals=0),
        name="column_panels",
    )(c0, c1, h0, r0, h1, r1, link)


ROWS = 256


def final_kernel(
    place_ref, base0_ref, base1_ref, rows_ref, cols_ref, low0_ref, low1_ref,
    h0_ref, r0_ref, h1_ref, r1_ref, link_ref, out_ref, left_ref,
):
    grid_row = place_ref[0]
    grid_column = place_ref[1]
    slot = pl.program_id(1)
    raw0 = rows_ref[:, 0, 0].reshape(ROWS, TILE)
    panel0 = mm(raw0, h0_ref[0], (1, 1)) + mm(raw0, r0_ref[0], (1, 1))
    round0 = panel0.astype(BF16)
    left1 = rows_ref[:, 1, 0].reshape(ROWS, TILE).astype(F32) - mm(round0, link_ref[0], (1, 1))
    high, rest = halves(left1)
    panel1 = mm(high, h1_ref[0], (1, 1)) + mm(rest, h1_ref[0], (1, 1)) + mm(high, r1_ref[0], (1, 1))
    round1 = panel1.astype(BF16)
    top = (slot == 0) & (grid_row < 2)
    for b, base_ref in enumerate((base0_ref, base1_ref)):
        span = slice(b * TILE, (b + 1) * TILE)
        update = mm(round0, cols_ref[0, :TILE, span]) + mm(round1, cols_ref[0, TILE:, span])
        value = jnp.where(top, 0.0, base_ref[0].astype(F32) - update)
        for j in range(4):
            out_ref[pl.ds(4 * b + j, ROWS, stride=8), :] = value[:, 128 * j : 128 * (j + 1)]

    @pl.when(grid_column == 0)
    def _():
        first = jnp.where((slot == 0) & (grid_row == 0), low0_ref[0], panel0)
        for j in range(4):
            out_ref[pl.ds(j, ROWS, stride=8), :] = first[:, 128 * j : 128 * (j + 1)]

    @pl.when(grid_column == 1)
    def _():
        second = jnp.where((slot == 0) & (grid_row == 0), 0.0, panel1)
        second = jnp.where((slot == 0) & (grid_row == 1), low1_ref[0], second)
        for j in range(4):
            out_ref[pl.ds(j, ROWS, stride=8), :] = second[:, 128 * j : 128 * (j + 1)]


def final_update(place, base0, base1, rows, cols, low0, low1, h0, r0, h1, r1, link):
    height = base0.shape[1]
    slots = height // TILE
    per = TILE // ROWS
    block = lambda w: pl.BlockSpec((1, ROWS, w), lambda c, a, s: (c, a * per + s, 0))
    tall = pl.BlockSpec((1, TILE, TILE), lambda c, a, s: (c, 0, 0))
    low = pl.BlockSpec((1, ROWS, TILE), lambda c, a, s: (c, s, 0))
    out = pl.pallas_call(
        final_kernel,
        grid=(CAND, slots, per),
        out_shape=jax.ShapeDtypeStruct((CAND * height * 8, 128), F32),
        in_specs=[
            pl.BlockSpec(memory_space=pltpu.SMEM),
            block(TILE),
            block(TILE),
            pl.BlockSpec((ROWS // 128, 2, 1, 128, TILE), lambda c, a, s: (a * per + s, 0, c, 0, 0)),
            pl.BlockSpec((1, 2 * TILE, 2 * TILE), lambda c, a, s: (c, 0, 0)),
            low,
            low,
            tall, tall, tall, tall, tall,
        ],
        out_specs=pl.BlockSpec((ROWS * 8, 128), lambda c, a, s: ((c * slots + a) * per + s, 0)),
        scratch_shapes=[pltpu.VMEM((8, 128), F32)],
        compiler_params=pltpu.CompilerParams(vmem_limit_bytes=50 * 2**20),
        cost_estimate=pl.CostEstimate(flops=21_500_000_000, bytes_accessed=40_000_000, transcendentals=0),
        name="final_update",
    )(place, base0, base1, rows, cols, low0, low1, h0, r0, h1, r1, link)
    return out


BOTH = ("prow", "pcol")
XS, ZS, YS = 4, 4, 4


def send(value, pairs):
    return lax.ppermute(value, BOTH, [(a[0] * 16 + a[1], b[0] * 16 + b[1]) for a, b in pairs])


def after(value, *earlier):
    return lax.optimization_barrier((value,) + earlier)[0]


def around_x(piece):
    return [
        send(
            piece,
            [
                ((p, w * XS + i), (p, w * XS + (i + k) % XS))
                for p in range(8) for w in range(ZS) for i in range(XS)
            ],
        )
        for k in range(1, XS)
    ]


def ring_spread(value, position, core, place, *gate):
    def pairs(core_index, source, target):
        return [
            ((a[0] * 2 + core_index, a[1]), (b[0] * 2 + core_index, b[1]))
            for a, b in zip(place(source), place(target))
        ]

    got = send(value, pairs(0, 0, 1) + pairs(1, 0, 3))
    if gate:
        got = after(got, *gate)
    value = jnp.where(position == jnp.where(core == 0, 1, 3), got, value)
    got = send(value, pairs(0, 0, 3) + pairs(0, 1, 2) + pairs(1, 0, 1) + pairs(1, 3, 2))
    last = (position == 2) | (position == jnp.where(core == 0, 3, 1))
    return jnp.where(last, got, value)


def chip(z, x):
    return z % ZS * XS + x % XS


def scatter_plan(s):
    east = [chip(0, s + 1), chip(1, s + 1), chip(3, s + 1), chip(2, s + 1)]
    west = [chip(0, s - 1), chip(1, s - 1), chip(3, s - 1), chip(2, s - 1)]
    north = [chip(1, s), chip(2, s), chip(1, s + 2), chip(2, s + 2)]
    south = [chip(3, s), None, chip(3, s + 2), chip(0, s + 2)]
    return [east, west, north, south]


def core_swap(value):
    return send(value, [((p, q), (p ^ 1, q)) for p in range(8) for q in range(16)])


def shards(covariance):
    height = 4 * TILE
    grid_row = lax.axis_index("prow")
    grid_column = lax.axis_index("pcol")
    core = grid_row % 2
    x = grid_column % XS
    z = grid_column // XS
    y = grid_row // 2
    half = TILE // 2
    place = jnp.stack([grid_row, grid_column, x]).astype(jnp.int32)

    tiles = [covariance[:, :, 0, :, b, 0, :].reshape(CAND, height, TILE) for b in range(2)]
    corner = tiles[0][:, :TILE]
    lower = jnp.concatenate(
        [corner[:, :half, :half], corner[:, half:, :half], corner[:, half:, half:]], 1
    )
    share = 3 * TILE // 4
    halved = send(lower[:, share:], [((0, 0), (1, 0))])
    moved = send(lower, [((1, 1), (0, 0))])
    first = jnp.where(core == 0, lower[:, :share], halved)
    second = jnp.where(
        core == 0,
        jnp.concatenate([moved, lower[:, :half]], 1),
        jnp.concatenate([corner[:, :, :half], corner[:, :, half:]], 1),
    )

    def quarter(k):
        return jnp.concatenate(
            [
                first[:, k * share // XS : (k + 1) * share // XS],
                second[:, k * half : (k + 1) * half],
            ],
            1,
        )

    held = quarter(0)
    dealt = [send(quarter(k), [((c, 0), (c, k)) for c in range(2)]) for k in range(1, XS)]
    for k in range(1, XS):
        held = jnp.where(x == k, dealt[k - 1], held)

    pieces = tiles[0].reshape(CAND, 16, height // 16, TILE)
    plans = [scatter_plan(0), scatter_plan(1)]
    level1 = []
    messages = []
    for g in range(4):
        def message(s):
            members = [plans[s][g][0] if m is None else m for m in plans[s][g]]
            return jnp.stack([pieces[:, m] for m in members])
        value = jnp.where(grid_column == 0, message(0), message(1))
        messages.append(value)
        level1.append(
            lax.ppermute(after(value, *dealt), "pcol", [(s, plans[s][g][0]) for s in range(2)])
        )

    wide = jnp.concatenate([tiles[0][:, :TILE], tiles[1][:, :TILE]], 2)
    held = ring_spread(
        after(held, *messages), z, core, lambda i: [(0, i * XS + j) for j in range(XS)]
    )
    held = ring_spread(
        after(held, wide), y, core, lambda i: [(i, q) for q in range(16)]
    )

    holding = [[plans[s][g][0] for g in range(4)] for s in range(2)]
    level1 = list(lax.optimization_barrier((*level1, held)))[:4]
    group = level1[3]
    for g in range(3):
        mine = (grid_column == holding[0][g]) | (grid_column == holding[1][g])
        group = jnp.where(mine, level1[g], group)
    rank1 = grid_column == holding[1][0]
    for g in range(1, 4):
        rank1 = rank1 | (grid_column == holding[1][g])
    turns = [(1, 1), (2, 3), (3, 2)]
    level2 = []
    for i0, i1 in turns:
        value = jnp.where(rank1, group[i1], group[i0])
        pairs = [
            (plans[s][g][0], plans[s][g][i])
            for s, i in ((0, i0), (1, i1)) for g in range(4) if plans[s][g][i] is not None
        ]
        level2.append(lax.ppermute(value, "pcol", pairs))
    around0 = around_x(held[:, : share // XS])
    level2 = list(lax.optimization_barrier((*level2, *around0)))[:3]
    own = [pieces[:, 0], pieces[:, 1]]
    rows_held = []
    for s in range(2):
        value = own[s]
        for g in range(4):
            value = jnp.where(grid_column == plans[s][g][0], group[0], value)
            for n, turn in enumerate(turns):
                target = plans[s][g][turn[s]]
                if target is not None:
                    value = jnp.where(grid_column == target, level2[n], value)
        rows_held.append(value)
    rows = lax.all_gather(jnp.stack(rows_held), "pcol", axis=0)

    own0 = jnp.stack([held[:, : share // XS]] + around0)
    other0 = core_swap(own0)
    later = after(held, other0)[:, share // XS :]
    around1 = around_x(later)

    column_place = lambda i: [(i, q) for q in range(16)]

    half_done = factor_first(place, own0, other0)
    own1 = jnp.stack(lax.optimization_barrier((later, *around1, half_done[2]))[:4])
    other1 = core_swap(own1)
    low0, inv0, h0, r0 = factor_rest(*half_done)
    mine = ring_spread(wide, y, core, column_place, half_done[2])
    half_next = factor_second(place, own1, other1, inv0)
    link = half_next[3]
    mine = after(mine, half_next[2])
    other = core_swap(mine)
    cols0 = jnp.where(core == 0, mine, other)
    cols1 = jnp.where(core == 0, other, mine)
    low1, _, h1, r1 = factor_rest(*half_next[:3])
    cols = column_panels(cols0, cols1, h0, r0, h1, r1, link)
    out = final_update(place, tiles[0], tiles[1], rows, cols, low0, low1, h0, r0, h1, r1, link)
    return out.reshape(covariance.shape)


def solution(mesh):
    spec = P(None, None, "prow", None, None, "pcol", None)
    return jax.shard_map(shards, mesh=mesh, in_specs=(spec,), out_specs=spec, check_vma=False)
```

```python
import jax
import jax.numpy as jnp
from jax import lax
from jax.experimental import pallas as pl
from jax.experimental.pallas import tpu as pltpu
from jax.sharding import PartitionSpec as P

TILE = 512
CAND = 2
BASE = 64
F32 = jnp.float32
BF16 = jnp.bfloat16


def lane_pick(value, column):
    lane = lax.broadcasted_iota(jnp.int32, (8, 128), 1)
    index = jnp.where(lane < BASE, column, BASE + column)
    return jnp.take_along_axis(value, index, axis=1, mode="promise_in_bounds")


def row_spread(value, row):
    return jnp.broadcast_to(value[row : row + 1, :], (8, 128))


def factor_base(groups):
    lane = lax.broadcasted_iota(jnp.int32, (8, 128), 1)
    half = jnp.where(lane < BASE, lane, lane - BASE)
    sub = lax.broadcasted_iota(jnp.int32, (8, 128), 0)
    work = list(groups)
    inverse = [jnp.where(half == sub + 8 * i, 1.0, 0.0).astype(F32) for i in range(8)]
    lower = [jnp.zeros((8, 128), F32) for _ in range(8)]
    for i in range(8):
        rows = [row_spread(work[i], j) for j in range(8)]
        inv_rows = [row_spread(inverse[i], j) for j in range(8)]
        entry = [
            [lane_pick(rows[j], 8 * i + m) if m >= j else None for m in range(8)] for j in range(8)
        ]
        factor = [[None] * 8 for _ in range(8)]
        scale = [None] * 8
        for j in range(8):
            scale[j] = lax.rsqrt(entry[j][j])
            for m in range(j + 1, 8):
                factor[m][j] = entry[j][m] * scale[j]
            for a in range(j + 1, 8):
                for b in range(a, 8):
                    entry[a][b] = entry[a][b] - factor[a][j] * factor[b][j]
            rows[j] = rows[j] * scale[j]
            inv_rows[j] = inv_rows[j] * scale[j]
            for m in range(j + 1, 8):
                rows[m] = rows[m] - factor[m][j] * rows[j]
                inv_rows[m] = inv_rows[m] - factor[m][j] * inv_rows[j]
        merged = inv_rows[0]
        for j in range(1, 8):
            merged = jnp.where(sub == j, inv_rows[j], merged)
        inverse[i] = merged
        for q in range(i, 8):
            column = [lane_pick(work[q], 8 * i + j) for j in range(8)]
            for j in range(8):
                column[j] = column[j] * scale[j]
                for m in range(j + 1, 8):
                    column[m] = column[m] - column[j] * factor[m][j]
                here = half == 8 * i + j
                if q == i:
                    here = here & (sub >= j)
                lower[q] = jnp.where(here, column[j], lower[q])
            if q > i:
                for j in range(8):
                    work[q] = work[q] - column[j] * rows[j]
                    inverse[q] = inverse[q] - column[j] * inv_rows[j]
    return lower, inverse


def dot_high(left, right, right_dim):
    return lax.dot_general(
        left,
        right,
        (((1,), (right_dim,)), ((), ())),
        precision=lax.Precision.HIGHEST,
        preferred_element_type=F32,
    )


def factor_bottom(work, low, inv, start, size):
    half = size // 2
    top = slice(start, start + half)
    bottom = slice(start + half, start + size)
    factor_block(work, low, inv, start + half, half)
    for c in range(CAND):
        inner = dot_high(low[c, bottom, top], inv[c, top, top], 0)
        inv[c, bottom, top] = -dot_high(inv[c, bottom, bottom], inner, 0)


def factor_top(work, low, inv, start, size):
    half = size // 2
    top = slice(start, start + half)
    bottom = slice(start + half, start + size)
    factor_block(work, low, inv, start, half)
    for c in range(CAND):
        below = dot_high(work[c, bottom, top], inv[c, top, top], 1)
        low[c, bottom, top] = below
        work[c, bottom, bottom] = work[c, bottom, bottom] - dot_high(below, below, 1)


def factor_block(work, low, inv, start, size):
    if size == BASE:
        window = start // 128 * 128
        odd = start % 128 != 0
        rows = slice(start, start + BASE)
        lane = lax.broadcasted_iota(jnp.int32, (BASE, 128), 1)
        first = work[0, rows, window : window + 128]
        second = work[1, rows, window : window + 128]
        if odd:
            first = pltpu.roll(first, BASE, 1)
        else:
            second = pltpu.roll(second, BASE, 1)
        both = jnp.where(lane < BASE, first, second)
        lower, inverse = factor_base([both[8 * i : 8 * i + 8, :] for i in range(8)])
        for target, parts in ((low, lower), (inv, inverse)):
            value = jnp.concatenate(parts, 0)
            rolled = pltpu.roll(value, BASE, 1)
            cols = slice(start, start + BASE)
            if odd:
                target[0, rows, cols] = rolled[:, BASE:]
                target[1, rows, cols] = value[:, BASE:]
            else:
                target[0, rows, cols] = value[:, :BASE]
                target[1, rows, cols] = rolled[:, :BASE]
        return
    factor_top(work, low, inv, start, size)
    factor_bottom(work, low, inv, start, size)


def split_store(inv, high_ref, rest_ref):
    for c in range(CAND):
        value = inv[c]
        high = value.astype(BF16)
        high_ref[c] = high
        rest_ref[c] = (value - high.astype(F32)).astype(BF16)


def unpack_lower(work, packed):
    half = TILE // 2
    for c in range(CAND):
        work[c, :half, :half] = packed[c, :half].astype(F32)
        work[c, half:, :half] = packed[c, half : 2 * half].astype(F32)
        work[c, half:, half:] = packed[c, 2 * half : 3 * half].astype(F32)


def sort_parts(place_ref, own_ref, other_ref, first, second, offset):
    step = own_ref.shape[2]
    odd = lax.rem(place_ref[0], 2)
    for k in range(4):
        start = lax.rem(place_ref[2] + 4 - k, 4) * step
        low = pl.ds(pl.multiple_of(start, 16), step)
        high = pl.ds(pl.multiple_of(start + offset, 16), step)

        @pl.when(odd == 0)
        def _():
            first[:, low, :] = own_ref[k]
            second[:, high, :] = other_ref[k]

        @pl.when(odd == 1)
        def _():
            first[:, low, :] = other_ref[k]
            second[:, high, :] = own_ref[k]


def first_kernel(place_ref, own_ref, other_ref, low_ref, inv_ref, work, packed):
    sort_parts(place_ref, own_ref, other_ref, packed, packed, 3 * TILE // 4)
    unpack_lower(work, packed)
    low_ref[...] = jnp.zeros_like(low_ref)
    inv_ref[...] = jnp.zeros_like(inv_ref)
    factor_top(work, low_ref, inv_ref, 0, TILE)


def rest_kernel(
    low_in, inv_in, work_in, low_ref, inv_ref, high_ref, rest_ref, work
):
    low_ref[...] = low_in[...]
    inv_ref[...] = inv_in[...]
    work[...] = work_in[...]
    factor_bottom(work, low_ref, inv_ref, 0, TILE)
    split_store(inv_ref, high_ref, rest_ref)


def second_kernel(
    place_ref, own_ref, other_ref, inv0_ref, low_ref, inv_ref, work, link_ref, diag, side
):
    low_ref[...] = jnp.zeros_like(low_ref)
    inv_ref[...] = jnp.zeros_like(inv_ref)
    sort_parts(place_ref, own_ref, other_ref, diag, side, 0)
    unpack_lower(work, diag)
    half = TILE // 2
    for c in range(CAND):
        panel = (
            dot_high(side[c, :TILE].astype(F32), inv0_ref[c, :, :half], 1)
            + dot_high(side[c, TILE:].astype(F32), inv0_ref[c, :, half:], 1)
        ).astype(BF16)
        link_ref[c] = panel
        work[c] = work[c] - lax.dot_general(
            panel, panel, (((1,), (1,)), ((), ())), preferred_element_type=F32
        )
    factor_top(work, low_ref, inv_ref, 0, TILE)


def whole(count):
    return [pl.BlockSpec(memory_space=pltpu.VMEM)] * count


def factor_first(place, own, other):
    shape = (CAND, TILE, TILE)
    return pl.pallas_call(
        first_kernel,
        out_shape=[jax.ShapeDtypeStruct(shape, F32)] * 3,
        in_specs=[pl.BlockSpec(memory_space=pltpu.SMEM)] + whole(2),
        out_specs=whole(3),
        scratch_shapes=[pltpu.VMEM((CAND, 3 * TILE // 2, TILE // 2), BF16)],
        compiler_params=pltpu.CompilerParams(vmem_limit_bytes=40 * 2**20),
        cost_estimate=pl.CostEstimate(flops=10_000_000_000, bytes_accessed=8_000_000, transcendentals=0),
        name="factor_first",
    )(place, own, other)


def factor_rest(low, inv, work):
    shape = (CAND, TILE, TILE)
    return pl.pallas_call(
        rest_kernel,
        out_shape=[
            jax.ShapeDtypeStruct(shape, F32),
            jax.ShapeDtypeStruct(shape, F32),
            jax.ShapeDtypeStruct(shape, BF16),
            jax.ShapeDtypeStruct(shape, BF16),
        ],
        in_specs=whole(3),
        out_specs=whole(4),
        scratch_shapes=[pltpu.VMEM(shape, F32)],
        compiler_params=pltpu.CompilerParams(vmem_limit_bytes=40 * 2**20),
        cost_estimate=pl.CostEstimate(flops=10_000_000_000, bytes_accessed=8_000_000, transcendentals=0),
        name="factor_rest",
    )(low, inv, work)


def factor_second(place, own, other, inv0):
    shape = (CAND, TILE, TILE)
    return pl.pallas_call(
        second_kernel,
        out_shape=[jax.ShapeDtypeStruct(shape, F32)] * 3 + [jax.ShapeDtypeStruct(shape, BF16)],
        in_specs=[pl.BlockSpec(memory_space=pltpu.SMEM)] + whole(3),
        out_specs=whole(4),
        scratch_shapes=[
            pltpu.VMEM((CAND, 2 * TILE, TILE // 2), BF16),
            pltpu.VMEM((CAND, 2 * TILE, TILE // 2), BF16),
        ],
        compiler_params=pltpu.CompilerParams(vmem_limit_bytes=40 * 2**20),
        cost_estimate=pl.CostEstimate(flops=10_000_000_000, bytes_accessed=8_000_000, transcendentals=0),
        name="factor_second",
    )(place, own, other, inv0)


def mm(left, right, dims=(1, 0)):
    return lax.dot_general(
        left, right, (((dims[0],), (dims[1],)), ((), ())), preferred_element_type=F32
    )


def halves(value):
    high = value.astype(BF16)
    return high, (value - high.astype(F32)).astype(BF16)


def column_kernel(c0_ref, c1_ref, h0_ref, r0_ref, h1_ref, r1_ref, link_ref, out_ref):
    raw0 = c0_ref[0]
    panel0 = (mm(h0_ref[0], raw0) + mm(r0_ref[0], raw0)).astype(BF16)
    out_ref[0, :TILE, :] = panel0
    left1 = c1_ref[0].astype(F32) - mm(link_ref[0], panel0)
    high, rest = halves(left1)
    panel1 = mm(h1_ref[0], high) + mm(h1_ref[0], rest) + mm(r1_ref[0], high)
    out_ref[0, TILE:, :] = panel1.astype(BF16)


def column_panels(c0, c1, h0, r0, h1, r1, link):
    width = c0.shape[2]
    step = 512
    tall = pl.BlockSpec((1, TILE, TILE), lambda c, j: (c, 0, 0))
    wide = pl.BlockSpec((1, TILE, step), lambda c, j: (c, 0, j))
    return pl.pallas_call(
        column_kernel,
        grid=(CAND, width // step),
        out_shape=jax.ShapeDtypeStruct((CAND, 2 * TILE, width), BF16),
        in_specs=[wide, wide, tall, tall, tall, tall, tall],
        out_specs=pl.BlockSpec((1, 2 * TILE, step), lambda c, j: (c, 0, j)),
        compiler_params=pltpu.CompilerParams(vmem_limit_bytes=40 * 2**20),
        cost_estimate=pl.CostEstimate(flops=6_500_000_000, bytes_accessed=12_000_000, transcendentals=0),
        name="column_panels",
    )(c0, c1, h0, r0, h1, r1, link)


ROWS = 512


def final_kernel(
    place_ref, base0_ref, base1_ref, rows_ref, cols_ref, low0_ref, low1_ref,
    h0_ref, r0_ref, h1_ref, r1_ref, link_ref, out_ref, left_ref,
):
    grid_row = place_ref[0]
    grid_column = place_ref[1]
    slot = pl.program_id(1)
    raw0 = rows_ref[:, 0, 0].reshape(ROWS, TILE)
    panel0 = mm(raw0, h0_ref[0], (1, 1)) + mm(raw0, r0_ref[0], (1, 1))
    round0 = panel0.astype(BF16)
    left1 = rows_ref[:, 1, 0].reshape(ROWS, TILE).astype(F32) - mm(round0, link_ref[0], (1, 1))
    high, rest = halves(left1)
    panel1 = mm(high, h1_ref[0], (1, 1)) + mm(rest, h1_ref[0], (1, 1)) + mm(high, r1_ref[0], (1, 1))
    round1 = panel1.astype(BF16)
    top = (slot == 0) & (grid_row < 2)
    for b, base_ref in enumerate((base0_ref, base1_ref)):
        span = slice(b * TILE, (b + 1) * TILE)
        update = mm(round0, cols_ref[0, :TILE, span]) + mm(round1, cols_ref[0, TILE:, span])
        value = jnp.where(top, 0.0, base_ref[0].astype(F32) - update)
        for j in range(4):
            out_ref[pl.ds(4 * b + j, ROWS, stride=8), :] = value[:, 128 * j : 128 * (j + 1)]

    @pl.when(grid_column == 0)
    def _():
        first = jnp.where((slot == 0) & (grid_row == 0), low0_ref[0], panel0)
        for j in range(4):
            out_ref[pl.ds(j, ROWS, stride=8), :] = first[:, 128 * j : 128 * (j + 1)]

    @pl.when(grid_column == 1)
    def _():
        second = jnp.where((slot == 0) & (grid_row == 0), 0.0, panel1)
        second = jnp.where((slot == 0) & (grid_row == 1), low1_ref[0], second)
        for j in range(4):
            out_ref[pl.ds(j, ROWS, stride=8), :] = second[:, 128 * j : 128 * (j + 1)]


def final_update(place, base, rows, cols, low0, low1, h0, r0, h1, r1, link):
    height = base.shape[1]
    slots = height // TILE
    per = TILE // ROWS
    block = lambda b: pl.BlockSpec((1, ROWS, TILE), lambda c, a, s: (c, a * per + s, b))
    tall = pl.BlockSpec((1, TILE, TILE), lambda c, a, s: (c, 0, 0))
    low = pl.BlockSpec((1, ROWS, TILE), lambda c, a, s: (c, s, 0))
    out = pl.pallas_call(
        final_kernel,
        grid=(CAND, slots, per),
        out_shape=jax.ShapeDtypeStruct((CAND * height * 8, 128), F32),
        in_specs=[
            pl.BlockSpec(memory_space=pltpu.SMEM),
            block(0),
            block(1),
            pl.BlockSpec((ROWS // 128, 2, 1, 128, TILE), lambda c, a, s: (a * per + s, 0, c, 0, 0)),
            pl.BlockSpec((1, 2 * TILE, 2 * TILE), lambda c, a, s: (c, 0, 0)),
            low,
            low,
            tall, tall, tall, tall, tall,
        ],
        out_specs=pl.BlockSpec((ROWS * 8, 128), lambda c, a, s: ((c * slots + a) * per + s, 0)),
        scratch_shapes=[pltpu.VMEM((8, 128), F32)],
        compiler_params=pltpu.CompilerParams(vmem_limit_bytes=50 * 2**20),
        cost_estimate=pl.CostEstimate(flops=21_500_000_000, bytes_accessed=40_000_000, transcendentals=0),
        name="final_update",
    )(place, base, base, rows, cols, low0, low1, h0, r0, h1, r1, link)
    return out


BOTH = ("prow", "pcol")
XS, ZS, YS = 4, 4, 4


def send(value, pairs):
    return lax.ppermute(value, BOTH, [(a[0] * 16 + a[1], b[0] * 16 + b[1]) for a, b in pairs])


def after(value, *earlier):
    return lax.optimization_barrier((value,) + earlier)[0]


def around_x(piece):
    return [
        send(
            piece,
            [
                ((p, w * XS + i), (p, w * XS + (i + k) % XS))
                for p in range(8) for w in range(ZS) for i in range(XS)
            ],
        )
        for k in range(1, XS)
    ]


def ring_spread(value, position, core, place, *gate):
    def pairs(core_index, source, target):
        return [
            ((a[0] * 2 + core_index, a[1]), (b[0] * 2 + core_index, b[1]))
            for a, b in zip(place(source), place(target))
        ]

    got = send(value, pairs(0, 0, 1) + pairs(1, 0, 3))
    if gate:
        got = after(got, *gate)
    value = jnp.where(position == jnp.where(core == 0, 1, 3), got, value)
    got = send(value, pairs(0, 0, 3) + pairs(0, 1, 2) + pairs(1, 0, 1) + pairs(1, 3, 2))
    last = (position == 2) | (position == jnp.where(core == 0, 3, 1))
    return jnp.where(last, got, value)


def chip(z, x):
    return z % ZS * XS + x % XS


def scatter_plan(s):
    east = [chip(0, s + 1), chip(1, s + 1), chip(3, s + 1), chip(2, s + 1)]
    west = [chip(0, s - 1), chip(1, s - 1), chip(3, s - 1), chip(2, s - 1)]
    north = [chip(1, s), chip(2, s), chip(1, s + 2), chip(2, s + 2)]
    south = [chip(3, s), None, chip(3, s + 2), chip(0, s + 2)]
    return [east, west, north, south]


def core_swap(value):
    return send(value, [((p, q), (p ^ 1, q)) for p in range(8) for q in range(16)])


def shards(covariance):
    height = 4 * TILE
    grid_row = lax.axis_index("prow")
    grid_column = lax.axis_index("pcol")
    core = grid_row % 2
    x = grid_column % XS
    z = grid_column // XS
    y = grid_row // 2
    half = TILE // 2
    place = jnp.stack([grid_row, grid_column, x]).astype(jnp.int32)

    corner = covariance[:, 0, 0, :, 0, 0, :]
    lower = jnp.concatenate(
        [corner[:, :half, :half], corner[:, half:, :half], corner[:, half:, half:]], 1
    )
    share = 3 * TILE // 4
    halved = send(lower[:, share:], [((0, 0), (1, 0))])
    moved = send(lower, [((1, 1), (0, 0))])
    base = covariance.reshape(CAND, height, 2 * TILE)
    first = jnp.where(core == 0, lower[:, :share], halved)
    second = jnp.where(
        core == 0,
        jnp.concatenate([moved, lower[:, :half]], 1),
        jnp.concatenate([corner[:, :, :half], corner[:, :, half:]], 1),
    )

    def quarter(k):
        return jnp.concatenate(
            [
                first[:, k * share // XS : (k + 1) * share // XS],
                second[:, k * half : (k + 1) * half],
            ],
            1,
        )

    held = quarter(0)
    dealt = [send(quarter(k), [((c, 0), (c, k)) for c in range(2)]) for k in range(1, XS)]
    for k in range(1, XS):
        held = jnp.where(x == k, dealt[k - 1], held)

    pieces = base[:, :, :TILE].reshape(CAND, 16, height // 16, TILE)
    plans = [scatter_plan(0), scatter_plan(1)]
    level1 = []
    messages = []
    for g in range(4):
        def message(s):
            members = [plans[s][g][0] if m is None else m for m in plans[s][g]]
            return jnp.stack([pieces[:, m] for m in members])
        value = jnp.where(grid_column == 0, message(0), message(1))
        messages.append(value)
        level1.append(
            lax.ppermute(after(value, *dealt), "pcol", [(s, plans[s][g][0]) for s in range(2)])
        )

    wide = base[:, :TILE]
    held = ring_spread(
        after(held, *messages), z, core, lambda i: [(0, i * XS + j) for j in range(XS)]
    )
    held = ring_spread(
        held, y, core, lambda i: [(i, q) for q in range(16)], wide, *level1
    )

    holding = [[plans[s][g][0] for g in range(4)] for s in range(2)]
    level1 = list(lax.optimization_barrier((*level1, held)))[:4]
    group = level1[3]
    for g in range(3):
        mine = (grid_column == holding[0][g]) | (grid_column == holding[1][g])
        group = jnp.where(mine, level1[g], group)
    rank1 = grid_column == holding[1][0]
    for g in range(1, 4):
        rank1 = rank1 | (grid_column == holding[1][g])
    turns = [(1, 1), (2, 3), (3, 2)]
    level2 = []
    for i0, i1 in turns:
        value = jnp.where(rank1, group[i1], group[i0])
        pairs = [
            (plans[s][g][0], plans[s][g][i])
            for s, i in ((0, i0), (1, i1)) for g in range(4) if plans[s][g][i] is not None
        ]
        level2.append(lax.ppermute(value, "pcol", pairs))
    around0 = around_x(held[:, : share // XS])
    level2 = list(lax.optimization_barrier((*level2, *around0)))[:3]
    own = [pieces[:, 0], pieces[:, 1]]
    rows_held = []
    for s in range(2):
        value = own[s]
        for g in range(4):
            value = jnp.where(grid_column == plans[s][g][0], group[0], value)
            for n, turn in enumerate(turns):
                target = plans[s][g][turn[s]]
                if target is not None:
                    value = jnp.where(grid_column == target, level2[n], value)
        rows_held.append(value)
    rows = lax.all_gather(jnp.stack(rows_held), "pcol", axis=0)

    own0 = jnp.stack([held[:, : share // XS]] + around0)
    other0 = core_swap(own0)
    later = after(held, other0)[:, share // XS :]
    around1 = around_x(later)

    column_place = lambda i: [(i, q) for q in range(16)]

    half_done = factor_first(place, own0, other0)
    own1 = jnp.stack(lax.optimization_barrier((later, *around1, half_done[2]))[:4])
    other1 = core_swap(own1)
    low0, inv0, h0, r0 = factor_rest(*half_done)
    mine = ring_spread(wide, y, core, column_place, half_done[2])
    half_next = factor_second(place, own1, other1, inv0)
    link = half_next[3]
    mine = after(mine, half_next[2])
    other = core_swap(mine)
    cols0 = jnp.where(core == 0, mine, other)
    cols1 = jnp.where(core == 0, other, mine)
    low1, _, h1, r1 = factor_rest(*half_next[:3])
    cols = column_panels(cols0, cols1, h0, r0, h1, r1, link)
    out = final_update(place, base, rows, cols, low0, low1, h0, r0, h1, r1, link)
    return out.reshape(covariance.shape)


def solution(mesh):
    spec = P(None, None, "prow", None, None, "pcol", None)
    return jax.shard_map(shards, mesh=mesh, in_specs=(spec,), out_specs=spec, check_vma=False)
```
